1024 devices in a mesh: mp: 2 (over y_lo), row: 16 (over y_hi, x), col: 32 (over z, core).
Axes of the slice: x: 4, y: 8 (y_hi: 4, y_lo: 2; y = y_hi * 2 + y_lo), z: 16, core: 2. Of those that a mesh axis runs over, the one named last changes fastest.
Arguments:
- text_embeds: bfloat16 [160, 8192], P('row', 'col'), may hold values from -6 to 6
- image_embeds: bfloat16 [64, 8192], P(('mp', 'row'), 'col'), may hold values from -6 to 6
- offsets: int32 [4], replicated, may hold values from 0 to 16, as said below
- lengths: int32 [4], replicated, may hold values from 32 to 40
- loss_mask: int32 [160], P('row'), may hold values 0 or 1
- norm_gain: bfloat16 [2, 8192], P('mp', 'col'), may hold values from 0.5 to 1.5
- unembed_rows: bfloat16 [2, 160, 8192], P('mp', 'row', 'col'), may hold values from -0.0625 to 0.0625
- gate_up: bfloat16 [2, 8192, 2, 29568], P('mp', 'col', None, 'row'), may hold values from -0.0625 to 0.0625
- down_proj: bfloat16 [2, 29568, 8192], P('mp', 'row', 'col'), may hold values from -0.03125 to 0.03125
Outputs:
- dpo_loss: float32 [], replicated
- input_grad: float32 [160, 8192], P(('mp', 'row'), 'col')
The draws below stay inside these ranges and needn't reach their ends.
Inputs may be any that keep to these rules, and one draw needn't show every extreme that they name: Each sequence's image tokens end at least 8 positions before its end: offsets[s] + 24 <= 40. Tokens at or after lengths[s] are padding and never scored.
All inputs are finite; a program needn't handle non-finite values. No bound on the sum of `loss_mask` on one device may be relied on, other than what follows from the above.
Results may differ from the reference program's by a relative error of at most 0.035.
Values may be sent and summed in bfloat16 or wider, within the bound.
A program may use at most 32 MiB of HBM per device.

```python
import jax
import jax.numpy as jnp
from jax import lax

D = 8192
FF = 29568
SEQ = 40
IMG = 16
NSEQ = 4
TOKENS = 160
N_COL = 32


align_weight = 0.7


noise_weight = 0.71


clip_value = 0.0625


def embed_fields(key):
    text_key = jax.random.fold_in(key, 101)
    image_key = jax.random.fold_in(key, 202)
    text_field = jnp.clip(jax.random.normal(text_key, (TOKENS, D), jnp.float32), -6.0, 6.0)
    image_field = jnp.clip(jax.random.normal(image_key, (NSEQ * IMG, D), jnp.float32), -6.0, 6.0)
    return (text_field, image_field)


def offset_values(key):
    drawn_offsets = jax.random.randint(jax.random.fold_in(key, 303), (NSEQ,), 0, SEQ - IMG - 7, dtype=jnp.int32)
    shuffled = jax.random.permutation(jax.random.fold_in(key, 304), NSEQ)
    drawn_offsets = drawn_offsets.at[shuffled[0]].set(SEQ - IMG - 8)
    drawn_offsets = drawn_offsets.at[shuffled[1]].set(0)
    return drawn_offsets.astype(jnp.int32)


def draw_text_embeds(key, part):
    text_field, image_field = embed_fields(key)
    return text_field.astype(jnp.bfloat16)


def draw_image_embeds(key, part):
    text_field, image_field = embed_fields(key)
    return image_field.astype(jnp.bfloat16)


def draw_offsets(key, part):
    return offset_values(key)


def draw_unembed_rows(key, part):
    text_field, image_field = embed_fields(key)
    first_positions = offset_values(key)
    global_pos = jnp.arange(TOKENS, dtype=jnp.int32)
    position = global_pos % SEQ
    seq_id = global_pos // SEQ
    first_img = first_positions[seq_id]
    inside = (position >= first_img) & (position < first_img + IMG)
    source = jnp.clip(seq_id * IMG + position - first_img, 0, NSEQ * IMG - 1).astype(jnp.int32)
    placed = jnp.where(inside[:, None], jnp.take(image_field, source, axis=0), text_field)
    token_signs = (jax.random.randint(jax.random.fold_in(key, 405), (TOKENS,), 0, 2, dtype=jnp.int32) * 2 - 1).astype(jnp.float32)
    noise_key = jax.random.fold_in(key, 406)
    noise_field = jax.random.normal(noise_key, (2, TOKENS, D), jnp.float32)
    scale_factor = D ** (-0.5)
    aligned = align_weight * token_signs[:, None] * placed
    rows_value = scale_factor * (aligned[None, :, :] + noise_weight * noise_field)
    return jnp.clip(rows_value, -clip_value, clip_value).astype(jnp.bfloat16)


def plant(drawn, key, low, largest):
    index_at = [jax.random.randint(jax.random.fold_in(key, axis), (), 0, length) for axis, length in enumerate(drawn.shape)]
    longest = drawn.shape.index(max(drawn.shape))
    next_to = index_at[:longest] + [(index_at[longest] + 1) % drawn.shape[longest]] + index_at[longest + 1:]
    return drawn.at[tuple(index_at)].set(low).at[tuple(next_to)].set(largest)


def levels(rng, extent, shards, least, top_value):
    def one(dim, parts):
        draws = jax.random.uniform(jax.random.fold_in(jax.random.fold_in(rng, 6), dim), (parts,), jnp.float32, least / len(shards), top_value / len(shards))
        return jnp.repeat(jnp.exp(draws), extent[dim] // parts).reshape((-1,) + (1,) * (len(extent) - dim - 1))

    factor_of = one(*shards[0])
    for cut in shards[1:]:
        factor_of = factor_of * one(*cut)
    return factor_of


def scatter_about(stream_key, dims, spread, most, shards=(), kind=jnp.bfloat16):
    factor_of = levels(stream_key, dims, shards, -0.22, 0.18) if shards else 1.0
    array = jax.random.normal(stream_key, dims, jnp.float32) * spread * factor_of
    return jnp.minimum(jnp.maximum(array, -most), most).astype(kind)


def setup_inputs(seed: int = 0) -> dict:
    seeds = jax.random.split(jax.random.key(seed), 10)
    return {
        "text_embeds": draw_text_embeds(jax.random.fold_in(seeds[9], 71), 0),
        "image_embeds": draw_image_embeds(jax.random.fold_in(seeds[9], 71), 0),
        "offsets": draw_offsets(jax.random.fold_in(seeds[9], 71), 0),
        "lengths": plant(jax.random.randint(seeds[3], (NSEQ,), SEQ - 8, SEQ + 1), jax.random.fold_in(seeds[3], 1), SEQ - 8, SEQ).astype(jnp.int32),
        "loss_mask": plant((jax.random.randint(seeds[4], (TOKENS,), 0, 4) < 3).astype(jnp.int32), jax.random.fold_in(seeds[4], 1), 0, 1),
        "norm_gain": jnp.clip(1.0 + 0.1 * jax.random.normal(seeds[5], (2, D), jnp.float32), 0.5, 1.5).astype(jnp.bfloat16),
        "unembed_rows": draw_unembed_rows(jax.random.fold_in(seeds[9], 71), 0),
        "gate_up": scatter_about(seeds[7], (2, D, 2, FF), D ** -0.5, 0.0625, ((0, 2), (1, 32), (3, 16))),
        "down_proj": scatter_about(seeds[8], (2, FF, D), FF ** -0.5, 0.03125, ((0, 2), (1, 16), (2, 32))),
    }


dpo_beta = 0.1
norm_eps = 1e-06

def place_images(text_rows, images, offsets):
    tokens = text_rows.shape[0]
    global_pos = jnp.arange(tokens, dtype=jnp.int32)
    position = global_pos % SEQ
    seq_id = global_pos // SEQ
    first_img = offsets[seq_id]
    inside = (position >= first_img) & (position < first_img + IMG)
    source = jnp.clip(seq_id * IMG + position - first_img, 0, images.shape[0] - 1).astype(jnp.int32)
    return jnp.where(inside[:, None], jnp.take(images, source, axis=0), text_rows)

def dpo_terms(totals):
    policy = totals[0]
    frozen = totals[1]
    margin = policy[0::2] - frozen[0::2] - (policy[1::2] - frozen[1::2])
    loss_value = jnp.mean(jax.nn.softplus(-dpo_beta * margin))
    dmargin = -dpo_beta * jax.nn.sigmoid(-dpo_beta * margin) / margin.shape[0]
    return (loss_value, dmargin)

def gate_up_sums(inputs, weight):
    block_width = inputs.shape[1] // N_COL

    def add_block(running, block_id):
        columns = lax.dynamic_slice_in_dim(inputs, block_id * block_width, block_width, 1)
        weight_rows = lax.dynamic_slice_in_dim(weight, block_id * block_width, block_width, 0)
        partial_value = jnp.dot(columns, weight_rows, preferred_element_type=jnp.float32).astype(jnp.bfloat16)
        partial_value = lax.optimization_barrier(partial_value)
        return (running + partial_value.astype(jnp.float32), None)
    start_value = jnp.zeros((inputs.shape[0], weight.shape[1]), jnp.float32)
    running, unused = lax.scan(add_block, start_value, jnp.arange(N_COL, dtype=jnp.int32))
    return running

def reference(text_embeds, image_embeds, offsets, lengths, loss_mask, norm_gain, unembed_rows, gate_up, down_proj):
    inputs = place_images(text_embeds, image_embeds, offsets)
    tokens = inputs.shape[0]
    global_pos = jnp.arange(tokens, dtype=jnp.int32)
    position = global_pos % SEQ
    seq_id = global_pos // SEQ
    scored = ((position < lengths[seq_id]) & (loss_mask == 1)).astype(jnp.float32)
    saved = []
    seq_list = []
    for model_id in range(2):
        weight = gate_up[model_id].reshape(D, 2 * FF)
        pre_sums = gate_up_sums(inputs, weight)
        gate_part = pre_sums[:, :FF]
        up_part = pre_sums[:, FF:]
        hidden = (jax.nn.silu(gate_part) * up_part).astype(jnp.bfloat16)
        residual = inputs.astype(jnp.float32) + jnp.dot(hidden, down_proj[model_id], preferred_element_type=jnp.float32)
        coeff = norm_gain[model_id].astype(jnp.float32)[None, :] * unembed_rows[model_id].astype(jnp.float32)
        squares = lax.optimization_barrier(jnp.sum(residual * residual, axis=1))
        cross_term = lax.optimization_barrier(jnp.sum(residual * coeff, axis=1))
        inv_rms = lax.rsqrt(squares / D + norm_eps)
        tok_score = cross_term * inv_rms
        seq_list.append(lax.optimization_barrier(jnp.sum((scored * tok_score).reshape(-1, SEQ), axis=1)))
        saved.append((weight, gate_part, up_part, residual, coeff, cross_term, inv_rms))
    totals = jnp.stack(seq_list)
    loss_value, dmargin = dpo_terms(totals)
    weight, gate_part, up_part, residual, coeff, cross_term, inv_rms = saved[0]
    seq_grad = jnp.stack([dmargin, -dmargin], axis=1).reshape(-1)
    dscore = scored * jnp.repeat(seq_grad, SEQ)
    dresid = dscore[:, None] * (inv_rms[:, None] * coeff - (cross_term * inv_rms ** 3 / D)[:, None] * residual)
    dy_rows = dresid.astype(jnp.bfloat16)
    dhidden = jnp.dot(dy_rows, down_proj[0].T, preferred_element_type=jnp.float32)
    sigmoid_gate = jax.nn.sigmoid(gate_part)
    gate_grad = dhidden * up_part * sigmoid_gate * (1.0 + gate_part * (1.0 - sigmoid_gate))
    up_grad = dhidden * gate_part * sigmoid_gate
    pre_grad = jnp.concatenate([gate_grad, up_grad], axis=1).astype(jnp.bfloat16)
    input_grad = dresid + jnp.dot(pre_grad, weight.T, preferred_element_type=jnp.float32)
    return (loss_value, input_grad)
```

```python
import jax
import jax.numpy as jnp
from jax import lax
from jax.experimental import pallas as pl
from jax.experimental.pallas import tpu as pltpu
from jax.sharding import PartitionSpec as P

D = 8192
SEQ = 40
IMG = 16
ROWS = 16
CHIPS = 16
OWN = 10
HALF = 80
TILE = 128
TILES = 15
LAST = 56
BETA = 0.1
EPS = 1e-06
MESH = pl.DeviceIdType.MESH
LEADERS = (0, 3, -3, 6, -6)
F32 = jnp.float32
BF16 = jnp.bfloat16


def iota(shape, dim):
    return lax.broadcasted_iota(jnp.int32, shape, dim)


def dot(a, b, precision=None):
    return jnp.dot(a, b, preferred_element_type=F32, precision=precision)


def dot_t(a, b):
    return lax.dot_general(a, b, (((1,), (1,)), ((), ())), preferred_element_type=F32)


def kernel(
    text_ref,
    image_ref,
    offsets_ref,
    lengths_ref,
    mask_ref,
    gain_ref,
    unembed_ref,
    gate_up_ref,
    down_ref,
    loss_ref,
    grad_ref,
    w_s,
    d_s,
    tail_s,
    in_buf,
    un_buf,
    x_s,
    p_s,
    px_s,
    l1_s,
    lx_s,
    s_s,
    l2_s,
    h_s,
    q_s,
    qx_s,
    m1_s,
    mx_s,
    t_s,
    m2_s,
    g_s,
    gate_s,
    up_s,
    so_s,
    ro_s,
    res_buf,
    res_s,
    sum_buf,
    row_buf,
    sf_s,
    rf_s,
    w_sem,
    in_sem,
    un_sem,
    fx_sem,
    f1_sem,
    f2_sem,
    hz_sem,
    hc_sem,
    bx_sem,
    b1_sem,
    b2_sem,
    gz_sem,
    gc_sem,
    ro_sem,
    res_sem,
    sum_sem,
    row_sem,
    rf_sem,
):
    mp = lax.axis_index("mp")
    row = lax.axis_index("row")
    col = lax.axis_index("col")
    plane = mp * ROWS + row
    z = lax.div(col, 2)
    core = lax.rem(col, 2)

    def chip(offset):
        return lax.rem(z + offset + 2 * CHIPS, CHIPS)

    def at_chip(where):
        return {"col": 2 * where + core}

    def plane_id(index):
        return {"mp": lax.div(index, ROWS), "row": lax.rem(index, ROWS)}

    partner = {"col": 2 * z + 1 - core}

    def remote(src, dst, sems, index, device):
        return pltpu.make_async_remote_copy(
            src_ref=src,
            dst_ref=dst,
            send_sem=sems.at[0, index],
            recv_sem=sems.at[1, index],
            device_id=device,
            device_id_type=MESH,
        )

    def wait_bytes(ref, sem):
        pltpu.make_async_copy(ref, ref, sem).wait()

    w_copy = pltpu.make_async_copy(gate_up_ref, w_s, w_sem.at[0])
    d_copy = pltpu.make_async_copy(down_ref, d_s, w_sem.at[1])
    w_copy.start()
    d_copy.start()

    barrier = pltpu.get_barrier_semaphore()

    def greet_plane(d, carry):
        other = lax.rem(plane + d, 2 * ROWS)
        pl.semaphore_signal(barrier, inc=1, device_id=plane_id(other), device_id_type=MESH)
        return carry

    def greet_col(d, carry):
        other = lax.rem(col + d, 2 * CHIPS)
        pl.semaphore_signal(barrier, inc=1, device_id={"col": other}, device_id_type=MESH)
        return carry

    lax.fori_loop(1, 2 * ROWS, greet_plane, 0)
    lax.fori_loop(1, 2 * CHIPS, greet_col, 0)

    stage = jnp.concatenate(
        [
            text_ref[...].astype(F32),
            image_ref[...].astype(F32),
            jnp.zeros((4, text_ref.shape[1]), F32),
        ],
        axis=0,
    )
    in_buf[plane] = stage.astype(BF16)
    own_unembed = jnp.concatenate(
        [unembed_ref[...].astype(F32), jnp.zeros((6, text_ref.shape[1]), F32)], axis=0
    )
    un_buf[row] = own_unembed.astype(BF16)
    gain = gain_ref[...].astype(F32)
    pl.semaphore_wait(barrier, 2 * (2 * ROWS - 1))

    def to_plane(make):
        def send(d, carry):
            make(lax.rem(plane + d, 2 * ROWS)).start()
            return carry

        lax.fori_loop(1, 2 * ROWS, send, 0)

    def to_row(make):
        def send(d, carry):
            make(lax.rem(row + d, ROWS)).start()
            return carry

        lax.fori_loop(1, ROWS, send, 0)

    to_plane(lambda o: remote(in_buf.at[plane], in_buf.at[plane], in_sem, 0, plane_id(o)))
    to_row(lambda o: remote(un_buf.at[row], un_buf.at[row], un_sem, 0, {"row": o}))

    token = iota((SEQ * 4, 2 * ROWS * 16), 0)
    source = iota((SEQ * 4, 2 * ROWS * 16), 1)
    position = lax.rem(token, SEQ)
    seq_id = lax.div(token, SEQ)
    first = jnp.where(
        seq_id == 0,
        offsets_ref[0],
        jnp.where(seq_id == 1, offsets_ref[1], jnp.where(seq_id == 2, offsets_ref[2], offsets_ref[3])),
    )
    inside = (position >= first) & (position < first + IMG)
    image_row = seq_id * IMG + position - first
    from_image = lax.shift_right_arithmetic(image_row, 1) * 16 + OWN + (image_row & 1)
    from_text = (mp * ROWS + lax.div(token, OWN)) * 16 + lax.rem(token, OWN)
    pick = (source == jnp.where(inside, from_image, from_text)).astype(BF16)

    w_copy.wait()
    d_copy.wait()
    tail_s[...] = jnp.zeros_like(tail_s)
    start = (TILES - 1) * TILE
    tail_s[0, :LAST] = w_s[0, start:]
    tail_s[1, :LAST] = w_s[1, start:]
    tail_s[2, :LAST] = d_s[start:]

    def weight(j):
        if j == TILES - 1:
            return jnp.concatenate([tail_s[0], tail_s[1]], axis=0)
        rows = slice(j * TILE, (j + 1) * TILE)
        return jnp.concatenate([w_s[0, rows], w_s[1, rows]], axis=0)

    def down(j):
        return tail_s[2] if j == TILES - 1 else d_s[j * TILE : (j + 1) * TILE]

    wait_bytes(in_buf.at[pl.ds(0, 2 * ROWS - 1)], in_sem.at[1, 0])
    gathered = in_buf[...].reshape(2 * ROWS * 16, text_ref.shape[1])
    x_s[...] = dot(pick, gathered).astype(BF16)

    def reduce_start(partial, p, px, sx):
        for j in range(TILES):
            p[j] = partial(j).astype(BF16).reshape(2, HALF, p.shape[3])
            remote(p.at[j, 1 - core], px.at[j], sx, j, partner).start()

    def level_one():
        out = []
        for k, lead in enumerate(LEADERS):
            for side, o in enumerate((lead - 1, lead + 1)):
                out.append((o, lead, 2 * k + side))
        return sorted(out, key=lambda e: -abs(e[1]))

    def reduce_end(p, px, l1, lx, s, l2, sx, s1, s2):
        def pair(j):
            remote(p.at[j, 1 - core], px.at[j], sx, j, partner).wait_recv()
            return p[j, core].astype(F32) + px[j].astype(F32)

        def first_sum(o):
            j = chip(-o)

            def do(send):
                @pl.when(j != TILES)
                def _():
                    p[j, core] = pair(j).astype(BF16)
                    send(j)

            return do

        far = 2 - 4 * core
        first_sum(8)(lambda j: remote(p.at[j, core], lx, s1, 10, at_chip(chip(-far))).start())
        for o, lead, slot in level_one():
            first_sum(o)(
                lambda j, o=o, lead=lead, slot=slot: remote(
                    p.at[j, core], l1.at[slot], s1, slot, at_chip(chip(lead - o))
                ).start()
            )
        for k in (3, 4, 1, 2):
            lead = LEADERS[k]
            j = chip(-lead)

            @pl.when(j != TILES)
            def _(k=k, lead=lead, j=j):
                total = pair(j)
                for slot in (2 * k, 2 * k + 1):
                    remote(l1.at[slot], l1.at[slot], s1, slot, partner).wait_recv()
                    total = total + l1[slot].astype(F32)
                if abs(lead) == 6:
                    extra = core == (0 if lead == 6 else 1)

                    @pl.when(extra)
                    def _():
                        remote(lx, lx, s1, 10, partner).wait_recv()
                        s[k - 1] = (total + lx[...].astype(F32)).astype(BF16)

                    @pl.when(jnp.logical_not(extra))
                    def _():
                        s[k - 1] = total.astype(BF16)
                else:
                    s[k - 1] = total.astype(BF16)
                remote(s.at[k - 1], l2.at[k - 1], s2, k - 1, at_chip(j)).start()

    def reduce_final(p, px, l1, l2, sx, s1, s2):
        remote(p.at[z, 1 - core], px.at[z], sx, z, partner).wait_recv()
        total = p[z, core].astype(F32) + px[z].astype(F32)
        for slot in (0, 1):
            remote(l1.at[slot], l1.at[slot], s1, slot, partner).wait_recv()
            total = total + l1[slot].astype(F32)
        for k in range(4):
            remote(s_any(l2, k), s_any(l2, k), s2, k, partner).wait_recv()
            total = total + l2[k].astype(F32)
        return total

    def s_any(ref, k):
        return ref.at[k]

    def reduce_sent(p, px, l1, lx, s, l2, sx, s1, s2):
        for j in range(TILES):
            remote(p.at[j, 1 - core], px.at[j], sx, j, partner).wait_send()
        for o, slot in [(8, 10)] + [(o, slot) for o, _, slot in level_one()]:

            @pl.when(chip(-o) != TILES)
            def _(slot=slot):
                remote(lx, lx, s1, slot, partner).wait_send()

        for k in range(1, 5):

            @pl.when(chip(-LEADERS[k]) != TILES)
            def _(k=k):
                remote(lx, lx, s2, k - 1, partner).wait_send()

    def gather_all(g, sz, sc):
        sends = []

        def send(block, by, o, when):
            n = len(sends)
            pltpu.make_async_remote_copy(
                src_ref=g.at[block, core],
                dst_ref=g.at[block, core],
                send_sem=sz.at[0, n],
                recv_sem=sz.at[1, o + 7],
                device_id=at_chip(chip(by)),
                device_id_type=MESH,
            ).start()
            sends.append((n, when))

        def across(block):
            remote(g.at[block, core], g.at[block, core], sc, block, partner).start()

        mine = z != TILES

        @pl.when(mine)
        def _():
            for o in (6, -6, 3, -3, 1, -1):
                send(z, o, o, mine)
            across(z)

        for o in (1, -1, 3, -3, 6, -6, 2, -2, 4, -4, 5, -5, 7, -7, 8):
            block = chip(-o)
            there = block != TILES
            relays = core == (0 if o == 6 else 1)
            both = there & relays

            @pl.when(there)
            def _(o=o, block=block, there=there, relays=relays, both=both):
                pltpu.make_async_remote_copy(
                    src_ref=g.at[block, core],
                    dst_ref=g.at[block, core],
                    send_sem=sz.at[0, 0],
                    recv_sem=sz.at[1, o + 7],
                    device_id=partner,
                    device_id_type=MESH,
                ).wait_recv()
                if o in (3, -3, 6, -6):
                    if abs(o) == 6:

                        @pl.when(relays)
                        def _():
                            send(block, 2 if o == 6 else -2, 8, both)

                    send(block, 1, o + 1, there)
                    send(block, -1, o - 1, there)
                across(block)

        for j in range(TILES):
            remote(g.at[j, core], g.at[j, core], sc, j, partner).wait()
        for n, when in sends:

            @pl.when(when)
            def _(n=n):
                remote(g.at[0, 0], g.at[0, 0], sz, n, partner).wait_send()

    x = x_s[...]
    reduce_start(lambda j: dot_t(x, weight(j)), p_s, px_s, fx_sem)
    forward = (p_s, px_s, l1_s, lx_s, s_s, l2_s, fx_sem, f1_sem, f2_sem)
    reduce_end(*forward)

    @pl.when(z != TILES)
    def _():
        pre = reduce_final(p_s, px_s, l1_s, l2_s, fx_sem, f1_sem, f2_sem)
        gate = pre[:, :TILE]
        up = pre[:, TILE:]
        gate_s[...] = gate
        up_s[...] = up
        h_s[z, core] = (gate * jax.nn.sigmoid(gate) * up).astype(BF16)

    gather_all(h_s, hz_sem, hc_sem)

    def hidden(j):
        return h_s[j].reshape(2 * HALF, TILE)

    out = dot(hidden(TILES - 1), down(TILES - 1))
    for j in range(0, TILES - 1, 2):
        both = jnp.concatenate([hidden(j), hidden(j + 1)], axis=1)
        out = out + dot(both, d_s[j * TILE : (j + 2) * TILE])

    slot_row = iota((ROWS * 16, SEQ * 4), 0)
    slot_token = iota((ROWS * 16, SEQ * 4), 1)
    spread = (
        (slot_token == lax.div(slot_row, 16) * OWN + lax.rem(slot_row, 16)) & (lax.rem(slot_row, 16) < OWN)
    ).astype(BF16)
    so_s[...] = dot(spread, out.astype(BF16)).astype(BF16).reshape(so_s.shape)
    to_row(lambda o: remote(so_s.at[o], ro_s.at[row], ro_sem, 0, {"row": o}))
    ro_s[row] = so_s[row]
    own_row = iota((16, SEQ * 4), 0)
    own_pick = ((iota((16, SEQ * 4), 1) == row * OWN + own_row) & (own_row < OWN)).astype(BF16)
    own_rows = dot(own_pick, x)
    coeff = own_unembed * gain
    wait_bytes(ro_s.at[pl.ds(0, ROWS - 1)], ro_sem.at[1, 0])
    residual = own_rows + jnp.sum(ro_s[...].astype(F32), axis=0)
    res_s[...] = residual

    square = (iota((16, 128), 0) == iota((16, 128), 1)).astype(F32)

    def as_row(values):
        return jnp.sum(values * square, axis=0, keepdims=True)

    def as_column(values):
        return jnp.sum(values * square, axis=1, keepdims=True)

    sums = jnp.concatenate(
        [
            as_row(jnp.sum(residual * residual, axis=1, keepdims=True)),
            as_row(jnp.sum(residual * coeff, axis=1, keepdims=True)),
        ],
        axis=0,
    )
    sum_buf[col] = sums

    def send_sums(d, carry):
        other = lax.rem(col + d, 2 * CHIPS)
        remote(sum_buf.at[col], sum_buf.at[col], sum_sem, 0, {"col": other}).start()
        return carry

    lax.fori_loop(1, 2 * CHIPS, send_sums, 0)
    res_buf[row] = residual.astype(BF16)

    @pl.when(mp == 0)
    def _():
        to_row(lambda o: remote(res_buf.at[row], res_buf.at[row], res_sem, 0, {"row": o}))

    lane = iota((1, 128), 1)
    masked = jnp.zeros((1, 128), jnp.int32)
    for t in range(OWN):
        masked = jnp.where(lane == t, mask_ref[t], masked)
    place = lax.rem(row, 4) * OWN + lane
    scored = ((place < lengths_ref[lax.div(row, 4)]) & (masked == 1) & (lane < OWN)).astype(F32)

    wait_bytes(sum_buf.at[pl.ds(0, 2 * CHIPS - 1)], sum_sem.at[1, 0])
    totals = jnp.sum(sum_buf[...], axis=0)
    squares = totals[0:1]
    cross = totals[1:2]
    inv_rms = lax.rsqrt(squares / D + EPS)
    by_coeff = scored * inv_rms
    by_residual = scored * (cross * inv_rms * inv_rms * inv_rms / D)
    row_buf[plane] = jnp.concatenate(
        [scored * (cross * inv_rms), by_coeff, by_residual, jnp.zeros((1, 128), F32)], axis=0
    )
    to_plane(lambda o: remote(row_buf.at[plane], row_buf.at[plane], row_sem, 0, plane_id(o)))
    wait_bytes(row_buf.at[pl.ds(0, 2 * ROWS - 1)], row_sem.at[1, 0])

    margins = []
    for q in range(2):
        acc = jnp.zeros((1, 128), F32)
        for r in range(8):
            policy = row_buf[8 * q + r][0:1]
            frozen = row_buf[ROWS + 8 * q + r][0:1]
            acc = acc + (policy - frozen if r < 4 else frozen - policy)
        margins.append(jnp.sum(acc, axis=1, keepdims=True))
    logits = [-BETA * m for m in margins]
    losses = [jnp.maximum(v, 0.0) + jnp.log1p(jnp.exp(-jnp.abs(v))) for v in logits]
    loss_ref[...] = (losses[0] + losses[1]) * 0.5
    dmargin = [-BETA * jax.nn.sigmoid(v) * 0.5 for v in logits]

    @pl.when(mp == 0)
    def _():
        wait_bytes(un_buf.at[pl.ds(0, ROWS - 1)], un_sem.at[1, 0])
        wait_bytes(res_buf.at[pl.ds(0, ROWS - 1)], res_sem.at[1, 0])
        rows = []
        for r in range(ROWS):
            grad = dmargin[r // 8] if (r // 4) % 2 == 0 else -dmargin[r // 8]
            terms = row_buf[r]
            rows.append(
                (
                    (as_column(terms[1:2]) * grad) * (un_buf[r].astype(F32) * gain)
                    - (as_column(terms[2:3]) * grad) * res_buf[r].astype(F32)
                ).astype(BF16)
            )
        spread_rows = jnp.concatenate(rows, axis=0)
        token_row = iota((SEQ * 4, ROWS * 16), 0)
        token_slot = iota((SEQ * 4, ROWS * 16), 1)
        compact = (token_slot == lax.div(token_row, OWN) * 16 + lax.rem(token_row, OWN)).astype(BF16)
        dy = dot(compact, spread_rows).astype(BF16)

        reduce_start(lambda j: dot_t(dy, down(j)), q_s, qx_s, bx_sem)
        backward = (q_s, qx_s, m1_s, mx_s, t_s, m2_s, bx_sem, b1_sem, b2_sem)
        reduce_end(*backward)

        @pl.when(z != TILES)
        def _():
            dhidden = reduce_final(q_s, qx_s, m1_s, m2_s, bx_sem, b1_sem, b2_sem)
            gate = gate_s[...]
            up = up_s[...]
            sig = jax.nn.sigmoid(gate)
            gate_grad = dhidden * up * sig * (1.0 + gate * (1.0 - sig))
            up_grad = dhidden * gate * sig
            g_s[z, core] = jnp.concatenate([gate_grad, up_grad], axis=1).astype(BF16)

        gather_all(g_s, gz_sem, gc_sem)
        total = jnp.zeros((SEQ * 4, text_ref.shape[1]), F32)
        for j in range(TILES):
            total = total + dot(g_s[j].reshape(2 * HALF, 2 * TILE), weight(j))
        first_pair = jnp.where(lax.div(row, 8) == 0, dmargin[0], dmargin[1])
        own_grad = jnp.where(lax.rem(lax.div(row, 4), 2) == 0, first_pair, -first_pair)
        own_coeff = own_unembed * gain
        dresidual = (as_column(by_coeff) * own_grad) * own_coeff - (
            as_column(by_residual) * own_grad
        ) * res_s[...]
        back_slot = iota((SEQ * 4, 16), 1)
        back = ((iota((SEQ * 4, 16), 0) == row * OWN + back_slot) & (back_slot < OWN)).astype(F32)
        total = total + dot(back, dresidual, lax.Precision.HIGHEST)
        out_row = iota((2 * ROWS * 8, SEQ * 4), 0)
        out_token = iota((2 * ROWS * 8, SEQ * 4), 1)
        by_owner = (
            (out_token == lax.div(out_row, 8) * 5 + lax.rem(out_row, 8)) & (lax.rem(out_row, 8) < 5)
        ).astype(F32)
        sf_s[...] = dot(by_owner, total, lax.Precision.HIGHEST).reshape(sf_s.shape)
        to_plane(lambda o: remote(sf_s.at[o], rf_s.at[row], rf_sem, 0, plane_id(o)))
        rf_s[row] = sf_s[row]
        wait_bytes(rf_s.at[pl.ds(0, ROWS - 1)], rf_sem.at[1, 0])
        reduce_sent(*backward)
        wait_bytes(res_buf.at[pl.ds(0, ROWS - 1)], res_sem.at[0, 0])
        wait_bytes(sf_s.at[pl.ds(0, 2 * ROWS - 1)], rf_sem.at[0, 0])

    @pl.when(mp == 1)
    def _():
        wait_bytes(un_buf.at[pl.ds(0, ROWS - 1)], un_sem.at[1, 0])
        wait_bytes(rf_s, rf_sem.at[1, 0])

    grad_ref[...] = jnp.sum(rf_s[...], axis=0)[:5]
    reduce_sent(*forward)
    wait_bytes(in_buf.at[pl.ds(0, 2 * ROWS - 1)], in_sem.at[0, 0])
    wait_bytes(un_buf.at[pl.ds(0, ROWS - 1)], un_sem.at[0, 0])
    wait_bytes(ro_s.at[pl.ds(0, ROWS - 1)], ro_sem.at[0, 0])
    wait_bytes(sum_buf.at[pl.ds(0, 2 * CHIPS - 1)], sum_sem.at[0, 0])
    wait_bytes(row_buf.at[pl.ds(0, 2 * ROWS - 1)], row_sem.at[0, 0])


def local(
    text_embeds,
    image_embeds,
    offsets,
    lengths,
    loss_mask,
    norm_gain,
    unembed_rows,
    gate_up,
    down_proj,
):
    width = text_embeds.shape[1]
    units = down_proj.shape[1]
    vmem = pl.BlockSpec(memory_space=pltpu.VMEM)
    smem = pl.BlockSpec(memory_space=pltpu.SMEM)
    anywhere = pl.BlockSpec(memory_space=pl.ANY)
    sems = pltpu.SemaphoreType.DMA

    def half(*shape):
        return pltpu.VMEM(shape, BF16)

    def full(*shape):
        return pltpu.VMEM(shape, F32)

    loss, grad = pl.pallas_call(
        kernel,
        out_shape=(jax.ShapeDtypeStruct((1, 1), F32), jax.ShapeDtypeStruct((5, width), F32)),
        in_specs=[vmem, vmem, smem, smem, smem, vmem, vmem, anywhere, anywhere],
        out_specs=(vmem, vmem),
        scratch_shapes=[
            half(2, units, width),
            half(units, width),
            half(3, TILE, width),
            half(2 * ROWS, 16, width),
            half(ROWS, 16, width),
            half(SEQ * 4, width),
            half(TILES, 2, HALF, 2 * TILE),
            half(TILES, HALF, 2 * TILE),
            half(10, HALF, 2 * TILE),
            half(HALF, 2 * TILE),
            half(4, HALF, 2 * TILE),
            half(4, HALF, 2 * TILE),
            half(TILES, 2, HALF, TILE),
            half(TILES, 2, HALF, TILE),
            half(TILES, HALF, TILE),
            half(10, HALF, TILE),
            half(HALF, TILE),
            half(4, HALF, TILE),
            half(4, HALF, TILE),
            half(TILES, 2, HALF, 2 * TILE),
            full(HALF, TILE),
            full(HALF, TILE),
            half(ROWS, 16, width),
            half(ROWS, 16, width),
            half(ROWS, 16, width),
            full(16, width),
            full(2 * CHIPS, 2, 128),
            full(2 * ROWS, 4, 128),
            full(2 * ROWS, 8, width),
            full(ROWS, 8, width),
            sems((2,)),
            sems((2, 1)),
            sems((2, 1)),
            sems((2, TILES)),
            sems((2, 11)),
            sems((2, 4)),
            sems((2, 17)),
            sems((2, TILES)),
            sems((2, TILES)),
            sems((2, 11)),
            sems((2, 4)),
            sems((2, 17)),
            sems((2, TILES)),
            sems((2, 1)),
            sems((2, 1)),
            sems((2, 1)),
            sems((2, 1)),
            sems((2, 1)),
        ],
        compiler_params=pltpu.CompilerParams(
            collective_id=0, has_side_effects=True, vmem_limit_bytes=40 << 20
        ),
        name="dpo_block",
    )(
        text_embeds,
        image_embeds,
        offsets,
        lengths,
        loss_mask,
        norm_gain,
        unembed_rows[0],
        jnp.transpose(gate_up[0], (1, 2, 0)),
        down_proj[0],
    )
    return loss.reshape(()), grad


def solution(mesh):
    in_specs = (
        P("row", "col"),
        P(("mp", "row"), "col"),
        P(),
        P(),
        P("row"),
        P("mp", "col"),
        P("mp", "row", "col"),
        P("mp", "col", None, "row"),
        P("mp", "row", "col"),
    )
    out_specs = (P(), P(("mp", "row"), "col"))
    return jax.shard_map(local, mesh=mesh, in_specs=in_specs, out_specs=out_specs, check_vma=False)
```

```python
import jax
import jax.numpy as jnp
from jax import lax
from jax.experimental import pallas as pl
from jax.experimental.pallas import tpu as pltpu
from jax.sharding import PartitionSpec as P

D = 8192
SEQ = 40
IMG = 16
ROWS = 16
CHIPS = 16
OWN = 10
HALF = 80
TILE = 128
TILES = 15
LAST = 56
BETA = 0.1
EPS = 1e-06
MESH = pl.DeviceIdType.MESH
LEADERS = (0, 3, -3, 6, -6)
F32 = jnp.float32
BF16 = jnp.bfloat16


def iota(shape, dim):
    return lax.broadcasted_iota(jnp.int32, shape, dim)


def dot(a, b, precision=None):
    return jnp.dot(a, b, preferred_element_type=F32, precision=precision)


def dot_t(a, b):
    return lax.dot_general(a, b, (((1,), (1,)), ((), ())), preferred_element_type=F32)


def kernel(
    text_in,
    image_in,
    offsets_in,
    lengths_in,
    mask_in,
    gain_in,
    unembed_in,
    gate_up_ref,
    down_ref,
    loss_ref,
    grad_ref,
    text_ref,
    image_ref,
    offsets_ref,
    lengths_ref,
    mask_ref,
    gain_ref,
    unembed_ref,
    w_s,
    d_s,
    wt_s,
    dt_s,
    tx_buf,
    im_buf,
    un_buf,
    x_s,
    p_s,
    px_s,
    l1_s,
    lx_s,
    s_s,
    l2_s,
    h_s,
    q_s,
    qx_s,
    m1_s,
    mx_s,
    t_s,
    m2_s,
    ab_s,
    g_s,
    so_s,
    ro_s,
    res_buf,
    res_s,
    sum_s,
    pair_s,
    sum_buf,
    row_buf,
    dr_s,
    sf_s,
    rf_s,
    spread_s,
    compact_s,
    owner_s,
    w_sem,
    tx_sem,
    im_sem,
    un_sem,
    fx_sem,
    f1_sem,
    f2_sem,
    hz_sem,
    hc_sem,
    az_sem,
    ac_sem,
    bx_sem,
    b1_sem,
    b2_sem,
    gz_sem,
    gc_sem,
    ro_sem,
    res_sem,
    pair_sem,
    sum_sem,
    row_sem,
    rf_sem,
):
    mp = lax.axis_index("mp")
    row = lax.axis_index("row")
    col = lax.axis_index("col")
    plane = mp * ROWS + row
    z = lax.div(col, 2)
    core = lax.rem(col, 2)

    def chip(offset):
        return lax.rem(z + offset + 2 * CHIPS, CHIPS)

    def at_chip(where):
        return {"col": 2 * where + core}

    def plane_id(index):
        return {"mp": lax.div(index, ROWS), "row": lax.rem(index, ROWS)}

    partner = {"col": 2 * z + 1 - core}

    def remote(src, dst, sems, index, device):
        return pltpu.make_async_remote_copy(
            src_ref=src,
            dst_ref=dst,
            send_sem=sems.at[0, index],
            recv_sem=sems.at[1, index],
            device_id=device,
            device_id_type=MESH,
        )

    def wait_bytes(ref, sem):
        pltpu.make_async_copy(ref, ref, sem).wait()

    copies = [
        pltpu.make_async_copy(src, dst, w_sem.at[n])
        for n, (src, dst) in enumerate(
            (
                (gate_up_ref, w_s),
                (down_ref, d_s),
                (text_in, text_ref),
                (image_in, image_ref),
                (unembed_in, unembed_ref),
                (gain_in, gain_ref),
                (offsets_in, offsets_ref),
                (lengths_in, lengths_ref),
                (mask_in, mask_ref),
            )
        )
    ]
    for copy in copies[2:]:
        copy.start()
    for copy in copies[:2]:
        copy.start()

    barrier = pltpu.get_barrier_semaphore()

    def greet_plane(d, carry):
        other = lax.rem(plane + d, 2 * ROWS)
        pl.semaphore_signal(barrier, inc=1, device_id=plane_id(other), device_id_type=MESH)
        return carry

    def greet_col(d, carry):
        pl.semaphore_signal(barrier, inc=1, device_id=at_chip(chip(d)), device_id_type=MESH)
        return carry

    lax.fori_loop(1, CHIPS, greet_col, 0)
    lax.fori_loop(1, 2 * ROWS, greet_plane, 0)
    pl.semaphore_signal(barrier, inc=1, device_id=partner, device_id_type=MESH)

    for copy in copies[2:]:
        copy.wait()
    width = text_ref.shape[1]

    zeros = jnp.zeros((6, width), F32)
    tx_buf[row] = jnp.concatenate([text_ref[...].astype(F32), zeros], axis=0).astype(BF16)
    im_buf[plane] = image_ref[...]
    own_unembed = jnp.concatenate([unembed_ref[...].astype(F32), zeros], axis=0)
    un_buf[row] = own_unembed.astype(BF16)
    gain = gain_ref[...].astype(F32)

    tokens = SEQ * 4
    token = iota((tokens, 1), 0)
    position = lax.rem(token, SEQ)
    seq_id = lax.div(token, SEQ)
    first = jnp.where(
        seq_id == 0,
        offsets_ref[0],
        jnp.where(seq_id == 1, offsets_ref[1], jnp.where(seq_id == 2, offsets_ref[2], offsets_ref[3])),
    )
    inside = (position >= first) & (position < first + IMG)
    token_slot = lax.div(token, OWN) * 16 + lax.rem(token, OWN)
    from_text = jnp.where(inside, -1, token_slot)
    from_image = jnp.where(inside, seq_id * IMG + position - first, -1)
    pick_text = (iota((tokens, ROWS * 16), 1) == from_text).astype(BF16)
    pick_image = (iota((tokens, 4 * IMG), 1) == from_image).astype(BF16)

    slot = iota((ROWS * 16, 1), 0)
    slot_token = jnp.where((slot & 15) < OWN, lax.shift_right_arithmetic(slot, 4) * OWN + (slot & 15), -1)
    spread_s[...] = (iota((ROWS * 16, tokens), 1) == slot_token).astype(BF16)
    compact_s[...] = (iota((tokens, ROWS * 16), 1) == token_slot).astype(BF16)
    owner_token = jnp.where((slot & 7) < 5, lax.shift_right_arithmetic(slot, 3) * 5 + (slot & 7), -1)
    owner_s[...] = (iota((ROWS * 16, tokens), 1) == owner_token).astype(BF16)

    for copy in copies[:2]:
        copy.wait()

    def lay_tile(j, carry):
        rows = pl.ds(pl.multiple_of(j * TILE, TILE), TILE)
        wt_s[j, :TILE] = w_s[0, rows]
        wt_s[j, TILE:] = w_s[1, rows]
        dt_s[j] = d_s[rows]
        return carry

    lax.fori_loop(0, TILES - 1, lay_tile, 0)
    last = TILES - 1
    wt_s[last:] = jnp.zeros((2, 2 * TILE, width), BF16)
    dt_s[last:] = jnp.zeros((2, TILE, width), BF16)
    wt_s[last, :LAST] = w_s[0, last * TILE :]
    wt_s[last, TILE : TILE + LAST] = w_s[1, last * TILE :]
    dt_s[last, :LAST] = d_s[last * TILE :]

    pl.semaphore_wait(barrier, 2 * ROWS - 1 + CHIPS)

    def to_plane(make):
        def send(d, carry):
            make(lax.rem(plane + 1 + lax.rem(d + 6, 2 * ROWS - 1), 2 * ROWS)).start()
            return carry

        lax.fori_loop(0, 2 * ROWS - 1, send, 0)

    def to_row(make):
        def send(d, carry):
            make(lax.rem(row + 1 + lax.rem(d + 5, ROWS - 1), ROWS)).start()
            return carry

        lax.fori_loop(0, ROWS - 1, send, 0)

    def all_but_one(ref):
        return ref.at[pl.ds(0, ref.shape[0] - 1)]

    to_row(lambda o: remote(tx_buf.at[row], tx_buf.at[row], tx_sem, 0, {"row": o}))
    to_plane(lambda o: remote(im_buf.at[plane], im_buf.at[plane], im_sem, 0, plane_id(o)))
    wait_bytes(all_but_one(tx_buf), tx_sem.at[1, 0])
    texts = dot(pick_text, tx_buf[...].reshape(ROWS * 16, width))
    wait_bytes(all_but_one(im_buf), im_sem.at[1, 0])
    images = jnp.concatenate([im_buf[i].astype(F32) for i in range(2 * ROWS)], axis=0).astype(BF16)
    x_s[...] = (texts + dot(pick_image, images)).astype(BF16)

    far_group = (5, 7, -5, -7, 8, 6, -6)
    mid_group = (2, 4, -2, -4, 3, -3)
    near_group = (1, -1, 0)

    def leader_of(o):
        lead = min((l for l in LEADERS if abs(l - o) == 1), default=None, key=abs)
        k = LEADERS.index(lead)
        return lead, 2 * k + (0 if o < lead else 1)

    def reduce(partial, p, px, l1, lx, s, l2, sx, s1, s2, deep, between=lambda: None):
        def compute(group):
            for o in group:
                j = chip(-o)
                p[j] = partial(j).astype(BF16).reshape(2, HALF, p.shape[3])
                remote(p.at[j, 1 - core], px.at[j], sx, j, partner).start()

        def pair(j):
            remote(p.at[j, 1 - core], px.at[j], sx, j, partner).wait_recv()
            return p[j, core].astype(F32) + px[j].astype(F32)

        def first_sums(group):
            for o in group:
                if o in LEADERS:
                    continue
                j = chip(-o)
                if o == 8:
                    dst, index, target = lx, 10, chip(4 * core - 2)
                else:
                    lead, index = leader_of(o)
                    dst, target = l1.at[index], chip(lead - o)

                @pl.when(j != TILES)
                def _(j=j, dst=dst, index=index, target=target):
                    p[j, core] = pair(j).astype(BF16)
                    remote(p.at[j, core], dst, s1, index, at_chip(target)).start()

        def arrived(ref, sems, index):
            remote(ref, ref, sems, index, partner).wait_recv()
            return ref[...].astype(F32)

        compute(far_group)
        compute(mid_group)
        first_sums(far_group)
        compute(near_group)
        first_sums(mid_group)
        first_sums(near_group)
        between()
        for k in (3, 4, 1, 2):
            lead = LEADERS[k]
            j = chip(-lead)

            @pl.when(j != TILES)
            def _(k=k, lead=lead, j=j):
                total = pair(j)
                for slot in (2 * k, 2 * k + 1):
                    total = total + arrived(l1.at[slot], s1, slot)
                target = j
                if abs(lead) == 6:
                    extra = core == (0 if lead == 6 else 1)

                    @pl.when(extra)
                    def _():
                        s[k - 1] = (total + arrived(lx, s1, 10)).astype(BF16)

                    @pl.when(jnp.logical_not(extra))
                    def _():
                        s[k - 1] = total.astype(BF16)

                    if deep:
                        target = chip(-lead // 2)
                else:
                    if deep:
                        total = total + arrived(l2.at[k + 1], s2, k + 1)
                    s[k - 1] = total.astype(BF16)
                remote(s.at[k - 1], l2.at[k - 1], s2, k - 1, at_chip(target)).start()

        def final():
            total = pair(z)
            for slot in (0, 1):
                total = total + arrived(l1.at[slot], s1, slot)
            for k in range(2 if deep else 4):
                total = total + arrived(l2.at[k], s2, k)
            return total

        def sent():
            remote(p.at[TILES, 1 - core], px.at[TILES], sx, TILES, partner).wait_recv()
            for j in range(TILES + 1):
                remote(p.at[j, 1 - core], px.at[j], sx, j, partner).wait_send()
            for o in range(-7, 9):
                if o in LEADERS:
                    continue
                index = 10 if o == 8 else leader_of(o)[1]

                @pl.when(chip(-o) != TILES)
                def _(index=index):
                    remote(lx, lx, s1, index, partner).wait_send()

            for k in range(1, 5):

                @pl.when(chip(-LEADERS[k]) != TILES)
                def _(k=k):
                    remote(lx, lx, s2, k - 1, partner).wait_send()

        return final, sent

    mine = z != TILES

    def gather(g, sz, sc):
        sends = []

        def send(block, by, o, came, relay=None):
            n = len(sends)
            pltpu.make_async_remote_copy(
                src_ref=g.at[block, core],
                dst_ref=g.at[block, core],
                send_sem=sz.at[0, n],
                recv_sem=sz.at[1, o + 7],
                device_id=at_chip(chip(by)),
                device_id_type=MESH,
            ).start()
            sends.append((n, came, relay))

        def across(block):
            remote(g.at[block, core], g.at[block, core], sc, block, partner).start()

        def arrived(block, o):
            pltpu.make_async_remote_copy(
                src_ref=g.at[block, core],
                dst_ref=g.at[block, core],
                send_sem=sz.at[0, 0],
                recv_sem=sz.at[1, o + 7],
                device_id=partner,
                device_id_type=MESH,
            ).wait_recv()

        def begin():
            @pl.when(mine)
            def _():
                for o in (6, -6, 3, -3, 1, -1):
                    send(z, o, o, 0)
                across(z)

        def take(offsets):
            for o in offsets:
                block = chip(-o)
                there = block != TILES
                relay = 0 if o == 6 else 1

                @pl.when(there)
                def _(o=o, block=block, relay=relay):
                    arrived(block, o)
                    if o in LEADERS:
                        if abs(o) == 6:

                            @pl.when(core == relay)
                            def _():
                                send(block, 2 if o == 6 else -2, 8, o, relay)

                        send(block, 1, o + 1, o)
                        send(block, -1, o - 1, o)
                    across(block)

        def end():
            for j in range(TILES):
                remote(g.at[j, core], g.at[j, core], sc, j, partner).wait()

        def sent():
            for n, came, relay in sends:
                when = chip(-came) != TILES
                if relay is not None:
                    when = when & (core == relay)

                @pl.when(when)
                def _(n=n):
                    remote(g.at[0, 0], g.at[0, 0], sz, n, partner).wait_send()

        return begin, take, end, sent

    leads = (3, -3, 6, -6)
    others = (1, -1, 2, -2, 4, -4, 5, -5, 7, -7, 8)

    x = x_s[...]
    forward_final, forward_sent = reduce(
        lambda j: dot_t(x, wt_s[j]), p_s, px_s, l1_s, lx_s, s_s, l2_s, fx_sem, f1_sem, f2_sem, True
    )
    h_begin, h_take, h_end, h_sent = gather(h_s, hz_sem, hc_sem)

    @pl.when(mine)
    def _():
        pre = forward_final()
        gate = pre[:, :TILE]
        up = pre[:, TILE:]
        sig = jax.nn.sigmoid(gate)
        silu = gate * sig
        h_s[z, core] = (silu * up).astype(BF16)
        ab_s[z, core] = jnp.concatenate([up * sig * (1.0 + gate * (1.0 - sig)), silu], axis=1).astype(BF16)

    h_begin()
    h_take((1, -1) + leads)

    @pl.when(mp == 0)
    def _():
        to_row(lambda o: remote(un_buf.at[row], un_buf.at[row], un_sem, 0, {"row": o}))

    h_take(others[2:])
    h_end()

    def hidden(j):
        return h_s[j].reshape(2 * HALF, TILE)

    out = dot(hidden(TILES - 1), dt_s[TILES - 1])
    for j in range(0, TILES - 1, 2):
        both = jnp.concatenate([hidden(j), hidden(j + 1)], axis=1)
        out = out + dot(both, dt_s[j : j + 2].reshape(2 * TILE, width))
    so_s[...] = dot(spread_s[...], out.astype(BF16)).astype(BF16).reshape(so_s.shape)
    to_row(lambda o: remote(so_s.at[o], ro_s.at[row], ro_sem, 0, {"row": o}))
    ro_s[row] = so_s[row]
    a_begin, a_take, a_end, a_sent = gather(ab_s, az_sem, ac_sem)

    @pl.when(mp == 0)
    def _():
        a_begin()

    own_row = iota((16, tokens), 0)
    own_pick = ((iota((16, tokens), 1) == row * OWN + own_row) & (own_row < OWN)).astype(BF16)
    own_rows = dot(own_pick, x)
    coeff = own_unembed * gain
    wait_bytes(all_but_one(ro_s), ro_sem.at[1, 0])
    residual = own_rows + jnp.sum(ro_s[...].astype(F32), axis=0)
    res_s[...] = residual

    square = (iota((16, 128), 0) == iota((16, 128), 1)).astype(F32)

    def as_row(values):
        return jnp.sum(values * square, axis=0, keepdims=True)

    def as_column(values):
        return jnp.sum(values * square, axis=1, keepdims=True)

    sum_s[...] = jnp.concatenate(
        [
            as_row(jnp.sum(residual * residual, axis=1, keepdims=True)),
            as_row(jnp.sum(residual * coeff, axis=1, keepdims=True)),
        ],
        axis=0,
    )
    to_partner = remote(sum_s, pair_s, pair_sem, 0, partner)
    to_partner.start()
    res_buf[row] = residual.astype(BF16)
    lane = iota((1, 128), 1)
    masked = jnp.zeros((1, 128), jnp.int32)
    for t in range(OWN):
        masked = jnp.where(lane == t, mask_ref[t], masked)
    place = lax.rem(row, 4) * OWN + lane
    scored = ((place < lengths_ref[lax.div(row, 4)]) & (masked == 1) & (lane < OWN)).astype(F32)
    to_partner.wait_recv()
    sum_buf[z] = sum_s[...] + pair_s[...]

    def send_sums(d, carry):
        other = lax.rem(z + 1 + lax.rem(d + 5, CHIPS - 1), CHIPS)
        remote(sum_buf.at[z], sum_buf.at[z], sum_sem, 0, at_chip(other)).start()
        return carry

    lax.fori_loop(0, CHIPS - 1, send_sums, 0)

    @pl.when(mp == 0)
    def _():
        to_row(lambda o: remote(res_buf.at[row], res_buf.at[row], res_sem, 0, {"row": o}))

    wait_bytes(all_but_one(sum_buf), sum_sem.at[1, 0])
    totals = jnp.sum(sum_buf[...], axis=0)
    squares = totals[0:1]
    cross = totals[1:2]
    inv_rms = lax.rsqrt(squares / D + EPS)
    by_coeff = scored * inv_rms
    by_residual = scored * (cross * inv_rms * inv_rms * inv_rms / D)
    row_buf[plane] = jnp.concatenate(
        [scored * (cross * inv_rms), by_coeff, by_residual, jnp.zeros((1, 128), F32)], axis=0
    )
    to_plane(lambda o: remote(row_buf.at[plane], row_buf.at[plane], row_sem, 0, plane_id(o)))

    @pl.when(mp == 0)
    def _():
        a_take(leads)

    wait_bytes(all_but_one(row_buf), row_sem.at[1, 0])
    margins = []
    for q in range(2):
        acc = jnp.zeros((1, 128), F32)
        for r in range(8):
            policy = row_buf[8 * q + r][0:1]
            frozen = row_buf[ROWS + 8 * q + r][0:1]
            acc = acc + (policy - frozen if r < 4 else frozen - policy)
        margins.append(jnp.sum(acc, axis=1, keepdims=True))
    logits = [-BETA * m for m in margins]
    losses = [jnp.maximum(v, 0.0) + jnp.log1p(jnp.exp(-jnp.abs(v))) for v in logits]
    loss_ref[...] = (losses[0] + losses[1]) * 0.5
    dmargin = [-BETA * jax.nn.sigmoid(v) * 0.5 for v in logits]

    def two_parts(values):
        high = values.astype(BF16)
        return high, (values - high.astype(F32)).astype(BF16)

    @pl.when(mp == 0)
    def _():
        wait_bytes(all_but_one(un_buf), un_sem.at[1, 0])
        wait_bytes(all_but_one(res_buf), res_sem.at[1, 0])
        rows = []
        for r in range(ROWS):
            grad = dmargin[r // 8] if (r // 4) % 2 == 0 else -dmargin[r // 8]
            terms = row_buf[r]
            rows.append(
                (
                    (as_column(terms[1:2]) * grad) * (un_buf[r].astype(F32) * gain)
                    - (as_column(terms[2:3]) * grad) * res_buf[r].astype(F32)
                ).astype(BF16)
            )
        dy = dot(compact_s[...], jnp.concatenate(rows, axis=0)).astype(BF16)

        def between():
            a_take(others)
            first_pair = jnp.where(lax.div(row, 8) == 0, dmargin[0], dmargin[1])
            own_grad = jnp.where(lax.rem(lax.div(row, 4), 2) == 0, first_pair, -first_pair)
            dresidual = (as_column(by_coeff) * own_grad) * coeff - (
                as_column(by_residual) * own_grad
            ) * res_s[...]
            back_slot = iota((tokens, 16), 1)
            back = ((iota((tokens, 16), 0) == row * OWN + back_slot) & (back_slot < OWN)).astype(BF16)
            high, low = two_parts(dresidual)
            dr_s[...] = dot(back, high) + dot(back, low)

        backward_final, backward_sent = reduce(
            lambda j: dot_t(dy, dt_s[j]),
            q_s,
            qx_s,
            m1_s,
            mx_s,
            t_s,
            m2_s,
            bx_sem,
            b1_sem,
            b2_sem,
            False,
            between,
        )
        g_begin, g_take, g_end, g_sent = gather(g_s, gz_sem, gc_sem)

        @pl.when(mine)
        def _():
            g_s[z, core] = backward_final().astype(BF16)

        g_begin()
        g_take((1, -1) + leads)
        a_end()
        g_take(others[2:])
        g_end()
        total = dr_s[...]
        for j in range(TILES):
            dhidden = g_s[j].reshape(2 * HALF, TILE).astype(F32)
            factors = ab_s[j].reshape(2 * HALF, 2 * TILE).astype(F32)
            pre_grad = (jnp.concatenate([dhidden, dhidden], axis=1) * factors).astype(BF16)
            total = total + dot(pre_grad, wt_s[j])
        high, low = two_parts(total)
        by_owner = owner_s[...]
        sf_s[...] = (dot(by_owner, high) + dot(by_owner, low)).reshape(sf_s.shape)
        to_plane(lambda o: remote(sf_s.at[o], rf_s.at[row], rf_sem, 0, plane_id(o)))
        rf_s[row] = sf_s[row]
        backward_sent()
        a_sent()
        g_sent()
        wait_bytes(all_but_one(un_buf), un_sem.at[0, 0])
        wait_bytes(all_but_one(res_buf), res_sem.at[0, 0])
        wait_bytes(all_but_one(rf_s), rf_sem.at[1, 0])
        wait_bytes(all_but_one(sf_s), rf_sem.at[0, 0])

    @pl.when(mp == 1)
    def _():
        wait_bytes(rf_s, rf_sem.at[1, 0])

    grad_ref[...] = jnp.sum(rf_s[...], axis=0)[:5]
    forward_sent()
    h_sent()
    to_partner.wait_send()
    wait_bytes(all_but_one(tx_buf), tx_sem.at[0, 0])
    wait_bytes(all_but_one(im_buf), im_sem.at[0, 0])
    wait_bytes(all_but_one(ro_s), ro_sem.at[0, 0])
    wait_bytes(all_but_one(sum_buf), sum_sem.at[0, 0])
    wait_bytes(all_but_one(row_buf), row_sem.at[0, 0])


def local(
    text_embeds,
    image_embeds,
    offsets,
    lengths,
    loss_mask,
    norm_gain,
    unembed_rows,
    gate_up,
    down_proj,
):
    width = text_embeds.shape[1]
    units = down_proj.shape[1]
    vmem = pl.BlockSpec(memory_space=pltpu.VMEM)
    anywhere = pl.BlockSpec(memory_space=pl.ANY)
    sems = pltpu.SemaphoreType.DMA

    def half(*shape):
        return pltpu.VMEM(shape, BF16)

    def full(*shape):
        return pltpu.VMEM(shape, F32)

    def tree(units):
        return [
            half(TILES + 1, 2, HALF, units),
            half(TILES + 1, HALF, units),
            half(10, HALF, units),
            half(HALF, units),
            half(4, HALF, units),
            half(4, HALF, units),
        ]

    loss, grad = pl.pallas_call(
        kernel,
        out_shape=(jax.ShapeDtypeStruct((1, 1), F32), jax.ShapeDtypeStruct((5, width), F32)),
        in_specs=[anywhere] * 9,
        out_specs=(vmem, vmem),
        scratch_shapes=[
            half(*text_embeds.shape),
            half(*image_embeds.shape),
            pltpu.SMEM(offsets.shape, jnp.int32),
            pltpu.SMEM(lengths.shape, jnp.int32),
            pltpu.SMEM(loss_mask.shape, jnp.int32),
            half(*norm_gain.shape),
            half(*unembed_rows.shape[1:]),
            half(2, units, width),
            half(units, width),
            half(TILES + 1, 2 * TILE, width),
            half(TILES + 1, TILE, width),
            half(ROWS, 16, width),
            half(2 * ROWS, *image_embeds.shape),
            half(ROWS, 16, width),
            half(SEQ * 4, width),
            *tree(2 * TILE),
            half(TILES, 2, HALF, TILE),
            *tree(TILE),
            half(TILES + 1, 2, HALF, 2 * TILE),
            half(TILES, 2, HALF, TILE),
            half(ROWS, 16, width),
            half(ROWS, 16, width),
            half(ROWS, 16, width),
            full(16, width),
            full(2, 128),
            full(2, 128),
            full(CHIPS, 2, 128),
            full(2 * ROWS, 4, 128),
            full(SEQ * 4, width),
            full(2 * ROWS, 8, width),
            full(ROWS, 8, width),
            half(ROWS * 16, SEQ * 4),
            half(SEQ * 4, ROWS * 16),
            half(ROWS * 16, SEQ * 4),
            sems((9,)),
            sems((2, 1)),
            sems((2, 1)),
            sems((2, 1)),
            sems((2, TILES + 1)),
            sems((2, 11)),
            sems((2, 4)),
            sems((2, 17)),
            sems((2, TILES)),
            sems((2, 17)),
            sems((2, TILES)),
            sems((2, TILES + 1)),
            sems((2, 11)),
            sems((2, 4)),
            sems((2, 17)),
            sems((2, TILES)),
            *[sems((2, 1))] * 6,
        ],
        compiler_params=pltpu.CompilerParams(
            collective_id=0, has_side_effects=True, vmem_limit_bytes=60 << 20
        ),
        name="dpo_block",
    )(
        text_embeds,
        image_embeds,
        offsets,
        lengths,
        loss_mask,
        norm_gain,
        unembed_rows[0],
        jnp.transpose(gate_up[0], (1, 2, 0)),
        down_proj[0],
    )
    return loss.reshape(()), grad


def solution(mesh):
    in_specs = (
        P("row", "col"),
        P(("mp", "row"), "col"),
        P(),
        P(),
        P("row"),
        P("mp", "col"),
        P("mp", "row", "col"),
        P("mp", "col", None, "row"),
        P("mp", "row", "col"),
    )
    out_specs = (P(), P(("mp", "row"), "col"))
    return jax.shard_map(local, mesh=mesh, in_specs=in_specs, out_specs=out_specs, check_vma=False)
```

```python
import jax
import jax.numpy as jnp
from jax import lax
from jax.experimental import pallas as pl
from jax.experimental.pallas import tpu as pltpu
from jax.sharding import PartitionSpec as P

D = 8192
SEQ = 40
IMG = 16
ROWS = 16
CHIPS = 16
OWN = 10
HALF = 80
TILE = 128
TILES = 15
LAST = 56
BETA = 0.1
EPS = 1e-06
MESH = pl.DeviceIdType.MESH
LEADERS = (0, 3, -3, 6, -6)
F32 = jnp.float32
BF16 = jnp.bfloat16


def iota(shape, dim):
    return lax.broadcasted_iota(jnp.int32, shape, dim)


def dot(a, b, precision=None):
    return jnp.dot(a, b, preferred_element_type=F32, precision=precision)


def dot_t(a, b):
    return lax.dot_general(a, b, (((1,), (1,)), ((), ())), preferred_element_type=F32)


def kernel(
    text_in,
    image_in,
    offsets_in,
    lengths_in,
    mask_in,
    gain_in,
    unembed_in,
    gate_up_ref,
    down_ref,
    loss_ref,
    grad_ref,
    text_ref,
    image_ref,
    offsets_ref,
    lengths_ref,
    mask_ref,
    gain_ref,
    unembed_ref,
    w_s,
    d_s,
    wt_s,
    dt_s,
    tx_buf,
    im_buf,
    un_buf,
    x_s,
    p_s,
    px_s,
    l1_s,
    lx_s,
    s_s,
    l2_s,
    h_s,
    q_s,
    qx_s,
    m1_s,
    mx_s,
    t_s,
    m2_s,
    ab_s,
    g_s,
    so_s,
    ro_s,
    res_buf,
    res_s,
    sum_s,
    pair_s,
    sum_buf,
    row_buf,
    dr_s,
    sf_s,
    rf_s,
    spread_s,
    compact_s,
    owner_s,
    w_sem,
    tx_sem,
    im_sem,
    un_sem,
    fx_sem,
    f1_sem,
    f2_sem,
    hz_sem,
    hc_sem,
    az_sem,
    ac_sem,
    bx_sem,
    b1_sem,
    b2_sem,
    gz_sem,
    gc_sem,
    ro_sem,
    res_sem,
    pair_sem,
    sum_sem,
    row_sem,
    rf_sem,
):
    mp = lax.axis_index("mp")
    row = lax.axis_index("row")
    col = lax.axis_index("col")
    plane = mp * ROWS + row
    z = lax.div(col, 2)
    core = lax.rem(col, 2)

    def chip(offset):
        return lax.rem(z + offset + 2 * CHIPS, CHIPS)

    def at_chip(where):
        return {"col": 2 * where + core}

    def plane_id(index):
        return {"mp": lax.div(index, ROWS), "row": lax.rem(index, ROWS)}

    partner = {"col": 2 * z + 1 - core}

    def remote(src, dst, sems, index, device):
        return pltpu.make_async_remote_copy(
            src_ref=src,
            dst_ref=dst,
            send_sem=sems.at[0, index],
            recv_sem=sems.at[1, index],
            device_id=device,
            device_id_type=MESH,
        )

    def wait_bytes(ref, sem):
        pltpu.make_async_copy(ref, ref, sem).wait()

    copies = [
        pltpu.make_async_copy(src, dst, w_sem.at[n])
        for n, (src, dst) in enumerate(
            (
                (gate_up_ref, w_s),
                (down_ref, d_s),
                (text_in, text_ref),
                (image_in, image_ref),
                (unembed_in, unembed_ref),
                (gain_in, gain_ref),
                (offsets_in, offsets_ref),
                (lengths_in, lengths_ref),
                (mask_in, mask_ref),
            )
        )
    ]
    for copy in copies[2:]:
        copy.start()
    for copy in copies[:2]:
        copy.start()

    barrier = pltpu.get_barrier_semaphore()

    def greet_plane(d, carry):
        other = lax.rem(plane + d, 2 * ROWS)
        pl.semaphore_signal(barrier, inc=1, device_id=plane_id(other), device_id_type=MESH)
        return carry

    def greet_col(d, carry):
        pl.semaphore_signal(barrier, inc=1, device_id=at_chip(chip(d)), device_id_type=MESH)
        return carry

    lax.fori_loop(1, CHIPS, greet_col, 0)
    lax.fori_loop(1, 2 * ROWS, greet_plane, 0)
    pl.semaphore_signal(barrier, inc=1, device_id=partner, device_id_type=MESH)

    for copy in copies[2:]:
        copy.wait()
    width = text_ref.shape[1]

    zeros = jnp.zeros((6, width), F32)
    tx_buf[row] = jnp.concatenate(
        [text_ref[...].astype(F32), image_ref[...].astype(F32), zeros[:4]], axis=0
    ).astype(BF16)
    own_unembed = jnp.concatenate([unembed_ref[...].astype(F32), zeros], axis=0)
    un_buf[row] = own_unembed.astype(BF16)
    gain = gain_ref[...].astype(F32)

    pl.semaphore_wait(barrier, 2 * ROWS - 1 + CHIPS)

    def to_plane(make):
        def send(d, carry):
            make(lax.rem(plane + 1 + lax.rem(d + 6, 2 * ROWS - 1), 2 * ROWS)).start()
            return carry

        lax.fori_loop(0, 2 * ROWS - 1, send, 0)

    def to_row(make):
        def send(d, carry):
            make(lax.rem(row + 1 + lax.rem(d + 5, ROWS - 1), ROWS)).start()
            return carry

        lax.fori_loop(0, ROWS - 1, send, 0)

    def all_but_one(ref):
        return ref.at[pl.ds(0, ref.shape[0] - 1)]

    to_row(lambda o: remote(tx_buf.at[row], tx_buf.at[row], tx_sem, 0, {"row": o}))

    def send_image(d, carry):
        other = {"mp": 1 - mp, "row": lax.rem(row + 6 + d, ROWS)}
        remote(image_ref, im_buf.at[row], im_sem, 0, other).start()
        return carry

    lax.fori_loop(0, ROWS, send_image, 0)
    tokens = SEQ * 4
    token = iota((tokens, 1), 0)
    position = lax.rem(token, SEQ)
    seq_id = lax.div(token, SEQ)
    first = jnp.where(
        seq_id == 0,
        offsets_ref[0],
        jnp.where(seq_id == 1, offsets_ref[1], jnp.where(seq_id == 2, offsets_ref[2], offsets_ref[3])),
    )
    inside = (position >= first) & (position < first + IMG)
    token_slot = lax.div(token, OWN) * 16 + lax.rem(token, OWN)
    image_row = seq_id * IMG + position - first
    in_half = image_row - mp * (2 * IMG)
    near = (in_half >= 0) & (in_half < 2 * IMG)
    with_text = lax.shift_right_arithmetic(in_half, 1) * 16 + OWN + (in_half & 1)
    from_text = jnp.where(inside, jnp.where(near, with_text, -1), token_slot)
    from_image = jnp.where(inside & jnp.logical_not(near), image_row - (1 - mp) * (2 * IMG), -1)
    pick_text = (iota((tokens, ROWS * 16), 1) == from_text).astype(BF16)
    pick_image = (iota((tokens, 2 * IMG), 1) == from_image).astype(BF16)

    for copy in copies[:2]:
        copy.wait()

    def lay_tile(j, carry):
        rows = pl.ds(pl.multiple_of(j * TILE, TILE), TILE)
        wt_s[j, :TILE] = w_s[0, rows]
        wt_s[j, TILE:] = w_s[1, rows]
        dt_s[j] = d_s[rows]
        return carry

    lax.fori_loop(0, TILES - 1, lay_tile, 0)
    last = TILES - 1
    wt_s[last:] = jnp.zeros((2, 2 * TILE, width), BF16)
    dt_s[last:] = jnp.zeros((2, TILE, width), BF16)
    wt_s[last, :LAST] = w_s[0, last * TILE :]
    wt_s[last, TILE : TILE + LAST] = w_s[1, last * TILE :]
    dt_s[last, :LAST] = d_s[last * TILE :]

    wait_bytes(all_but_one(tx_buf), tx_sem.at[1, 0])
    texts = dot(pick_text, tx_buf[...].reshape(ROWS * 16, width))
    wait_bytes(im_buf, im_sem.at[1, 0])
    images = jnp.concatenate([im_buf[i].astype(F32) for i in range(ROWS)], axis=0).astype(BF16)
    x_s[...] = (texts + dot(pick_image, images)).astype(BF16)

    far_group = (5, 7, -5, -7, 8, 6, -6)
    mid_group = (2, 4, -2, -4, 3, -3)
    near_group = (1, -1, 0)
    order = far_group + mid_group + near_group

    def leader_of(o):
        lead = min((l for l in LEADERS if abs(l - o) == 1), default=None, key=abs)
        k = LEADERS.index(lead)
        return lead, 2 * k + (0 if o < lead else 1)

    def reduce(partial, p, px, l1, lx, s, l2, sx, s1, s2, deep, between=lambda: None):
        def compute(group):
            for o in group:
                n = order.index(o)
                p[n] = partial(chip(-o)).astype(BF16).reshape(2, HALF, p.shape[3])
                remote(p.at[n, 1 - core], px.at[n], sx, n, partner).start()

        def pair(o):
            n = order.index(o)
            remote(p.at[n, 1 - core], px.at[n], sx, n, partner).wait_recv()
            return p[n, core].astype(F32) + px[n].astype(F32)

        def first_sums(group):
            for o in group:
                if o in LEADERS:
                    continue
                j = chip(-o)
                if o == 8:
                    dst, index, target = lx, 10, chip(4 * core - 2)
                else:
                    lead, index = leader_of(o)
                    dst, target = l1.at[index], chip(lead - o)

                @pl.when(j != TILES)
                def _(o=o, dst=dst, index=index, target=target):
                    n = order.index(o)
                    p[n, core] = pair(o).astype(BF16)
                    remote(p.at[n, core], dst, s1, index, at_chip(target)).start()

        def arrived(ref, sems, index):
            remote(ref, ref, sems, index, partner).wait_recv()
            return ref[...].astype(F32)

        compute(far_group)
        compute(mid_group)
        first_sums(far_group)
        compute(near_group)
        first_sums(mid_group)
        first_sums(near_group)
        between()
        for k in (3, 4, 1, 2):
            lead = LEADERS[k]
            j = chip(-lead)

            @pl.when(j != TILES)
            def _(k=k, lead=lead, j=j):
                total = pair(lead)
                for slot in (2 * k, 2 * k + 1):
                    total = total + arrived(l1.at[slot], s1, slot)
                target = j
                if abs(lead) == 6:
                    extra = core == (0 if lead == 6 else 1)

                    @pl.when(extra)
                    def _():
                        s[k - 1] = (total + arrived(lx, s1, 10)).astype(BF16)

                    @pl.when(jnp.logical_not(extra))
                    def _():
                        s[k - 1] = total.astype(BF16)

                    if deep:
                        target = chip(-lead // 2)
                else:
                    if deep:
                        total = total + arrived(l2.at[k + 1], s2, k + 1)
                    s[k - 1] = total.astype(BF16)
                remote(s.at[k - 1], l2.at[k - 1], s2, k - 1, at_chip(target)).start()

        def final():
            total = pair(0)
            for slot in (0, 1):
                total = total + arrived(l1.at[slot], s1, slot)
            for k in range(2 if deep else 4):
                total = total + arrived(l2.at[k], s2, k)
            return total

        def sent():
            for n, o in enumerate(order):
                remote(p.at[n, 1 - core], px.at[n], sx, n, partner).wait_send()

                @pl.when(chip(-o) == TILES)
                def _(n=n):
                    remote(p.at[n, 1 - core], px.at[n], sx, n, partner).wait_recv()
            for o in range(-7, 9):
                if o in LEADERS:
                    continue
                index = 10 if o == 8 else leader_of(o)[1]

                @pl.when(chip(-o) != TILES)
                def _(index=index):
                    remote(lx, lx, s1, index, partner).wait_send()

            for k in range(1, 5):

                @pl.when(chip(-LEADERS[k]) != TILES)
                def _(k=k):
                    remote(lx, lx, s2, k - 1, partner).wait_send()

        return final, sent

    mine = z != TILES

    def gather(g, sz, sc):
        sends = []

        def send(block, by, o, came, relay=None):
            n = len(sends)
            pltpu.make_async_remote_copy(
                src_ref=g.at[block, core],
                dst_ref=g.at[block, core],
                send_sem=sz.at[0, n],
                recv_sem=sz.at[1, o + 7],
                device_id=at_chip(chip(by)),
                device_id_type=MESH,
            ).start()
            sends.append((n, came, relay))

        def across(block):
            remote(g.at[block, core], g.at[block, core], sc, block, partner).start()

        def arrived(block, o):
            pltpu.make_async_remote_copy(
                src_ref=g.at[block, core],
                dst_ref=g.at[block, core],
                send_sem=sz.at[0, 0],
                recv_sem=sz.at[1, o + 7],
                device_id=partner,
                device_id_type=MESH,
            ).wait_recv()

        def begin():
            @pl.when(mine)
            def _():
                for o in (6, -6, 3, -3, 1, -1):
                    send(z, o, o, 0)
                across(z)

        def take(offsets):
            for o in offsets:
                block = chip(-o)
                there = block != TILES
                relay = 0 if o == 6 else 1

                @pl.when(there)
                def _(o=o, block=block, relay=relay):
                    arrived(block, o)
                    if o in LEADERS:
                        if abs(o) == 6:

                            @pl.when(core == relay)
                            def _():
                                send(block, 2 if o == 6 else -2, 8, o, relay)

                        send(block, 1, o + 1, o)
                        send(block, -1, o - 1, o)
                    across(block)

        def end():
            for j in range(TILES):
                remote(g.at[j, core], g.at[j, core], sc, j, partner).wait()

        def sent():
            for n, came, relay in sends:
                when = chip(-came) != TILES
                if relay is not None:
                    when = when & (core == relay)

                @pl.when(when)
                def _(n=n):
                    remote(g.at[0, 0], g.at[0, 0], sz, n, partner).wait_send()

        return begin, take, end, sent

    leads = (3, -3, 6, -6)
    others = (1, -1, 2, -2, 4, -4, 5, -5, 7, -7, 8)

    def select():
        slot = iota((ROWS * 16, 1), 0)
        slot_token = jnp.where((slot & 15) < OWN, lax.shift_right_arithmetic(slot, 4) * OWN + (slot & 15), -1)
        spread_s[...] = (iota((ROWS * 16, tokens), 1) == slot_token).astype(BF16)
        compact_s[...] = (iota((tokens, ROWS * 16), 1) == token_slot).astype(BF16)
        owner_token = jnp.where((slot & 7) < 5, lax.shift_right_arithmetic(slot, 3) * 5 + (slot & 7), -1)
        owner_s[...] = (iota((ROWS * 16, tokens), 1) == owner_token).astype(BF16)

    x = x_s[...]
    forward_final, forward_sent = reduce(
        lambda j: dot_t(x, wt_s[j]), p_s, px_s, l1_s, lx_s, s_s, l2_s, fx_sem, f1_sem, f2_sem, False, select
    )
    h_begin, h_take, h_end, h_sent = gather(h_s, hz_sem, hc_sem)

    @pl.when(mine)
    def _():
        pre = forward_final()
        gate = pre[:, :TILE]
        up = pre[:, TILE:]
        sig = jax.nn.sigmoid(gate)
        silu = gate * sig
        h_s[z, core] = (silu * up).astype(BF16)
        ab_s[z, core] = jnp.concatenate([up * sig * (1.0 + gate * (1.0 - sig)), silu], axis=1).astype(BF16)

    h_begin()
    h_take(leads + (1, -1))

    @pl.when(mp == 0)
    def _():
        to_row(lambda o: remote(un_buf.at[row], un_buf.at[row], un_sem, 0, {"row": o}))

    h_take(others[2:])
    h_end()

    def hidden(j):
        return h_s[j].reshape(2 * HALF, TILE)

    out = dot(hidden(TILES - 1), dt_s[TILES - 1])
    for j in range(0, TILES - 1, 2):
        both = jnp.concatenate([hidden(j), hidden(j + 1)], axis=1)
        out = out + dot(both, dt_s[j : j + 2].reshape(2 * TILE, width))
    so_s[...] = dot(spread_s[...], out.astype(BF16)).astype(BF16).reshape(so_s.shape)
    to_row(lambda o: remote(so_s.at[o], ro_s.at[row], ro_sem, 0, {"row": o}))
    ro_s[row] = so_s[row]
    a_begin, a_take, a_end, a_sent = gather(ab_s, az_sem, ac_sem)

    @pl.when(mp == 0)
    def _():
        a_begin()

    own_row = iota((16, tokens), 0)
    own_pick = ((iota((16, tokens), 1) == row * OWN + own_row) & (own_row < OWN)).astype(BF16)
    own_rows = dot(own_pick, x)
    coeff = own_unembed * gain
    forward_sent()
    wait_bytes(all_but_one(ro_s), ro_sem.at[1, 0])
    residual = own_rows + jnp.sum(ro_s[...].astype(F32), axis=0)
    res_s[...] = residual

    square = (iota((16, 128), 0) == iota((16, 128), 1)).astype(F32)

    def as_row(values):
        return jnp.sum(values * square, axis=0, keepdims=True)

    def as_column(values):
        return jnp.sum(values * square, axis=1, keepdims=True)

    sum_s[...] = jnp.concatenate(
        [
            as_row(jnp.sum(residual * residual, axis=1, keepdims=True)),
            as_row(jnp.sum(residual * coeff, axis=1, keepdims=True)),
        ],
        axis=0,
    )
    to_partner = remote(sum_s, pair_s, pair_sem, 0, partner)
    to_partner.start()
    res_buf[row] = residual.astype(BF16)
    lane = iota((1, 128), 1)
    masked = jnp.zeros((1, 128), jnp.int32)
    for t in range(OWN):
        masked = jnp.where(lane == t, mask_ref[t], masked)
    place = lax.rem(row, 4) * OWN + lane
    scored = ((place < lengths_ref[lax.div(row, 4)]) & (masked == 1) & (lane < OWN)).astype(F32)
    to_partner.wait_recv()
    sum_buf[z] = sum_s[...] + pair_s[...]

    def send_sums(d, carry):
        other = lax.rem(z + 1 + lax.rem(d + 5, CHIPS - 1), CHIPS)
        remote(sum_buf.at[z], sum_buf.at[z], sum_sem, 0, at_chip(other)).start()
        return carry

    lax.fori_loop(0, CHIPS - 1, send_sums, 0)

    @pl.when(mp == 0)
    def _():
        to_row(lambda o: remote(res_buf.at[row], res_buf.at[row], res_sem, 0, {"row": o}))

    h_sent()
    to_partner.wait_send()
    wait_bytes(all_but_one(tx_buf), tx_sem.at[0, 0])
    wait_bytes(im_buf, im_sem.at[0, 0])
    wait_bytes(all_but_one(ro_s), ro_sem.at[0, 0])
    wait_bytes(all_but_one(sum_buf), sum_sem.at[1, 0])
    totals = jnp.sum(sum_buf[...], axis=0)
    squares = totals[0:1]
    cross = totals[1:2]
    inv_rms = lax.rsqrt(squares / D + EPS)
    by_coeff = scored * inv_rms
    by_residual = scored * (cross * inv_rms * inv_rms * inv_rms / D)
    row_buf[plane] = jnp.concatenate(
        [scored * (cross * inv_rms), by_coeff, by_residual, jnp.zeros((1, 128), F32)], axis=0
    )
    to_plane(lambda o: remote(row_buf.at[plane], row_buf.at[plane], row_sem, 0, plane_id(o)))

    @pl.when(mp == 0)
    def _():
        a_take(leads)

    wait_bytes(all_but_one(row_buf), row_sem.at[1, 0])
    margins = []
    for q in range(2):
        acc = jnp.zeros((1, 128), F32)
        for r in range(8):
            policy = row_buf[8 * q + r][0:1]
            frozen = row_buf[ROWS + 8 * q + r][0:1]
            acc = acc + (policy - frozen if r < 4 else frozen - policy)
        margins.append(jnp.sum(acc, axis=1, keepdims=True))
    logits = [-BETA * m for m in margins]
    losses = [jnp.maximum(v, 0.0) + jnp.log1p(jnp.exp(-jnp.abs(v))) for v in logits]
    loss_ref[...] = (losses[0] + losses[1]) * 0.5
    dmargin = [-BETA * jax.nn.sigmoid(v) * 0.5 for v in logits]

    def two_parts(values):
        high = values.astype(BF16)
        return high, (values - high.astype(F32)).astype(BF16)

    @pl.when(mp == 0)
    def _():
        wait_bytes(all_but_one(un_buf), un_sem.at[1, 0])
        wait_bytes(all_but_one(res_buf), res_sem.at[1, 0])
        rows = []
        for r in range(ROWS):
            grad = dmargin[r // 8] if (r // 4) % 2 == 0 else -dmargin[r // 8]
            terms = row_buf[r]
            rows.append(
                (
                    (as_column(terms[1:2]) * grad) * (un_buf[r].astype(F32) * gain)
                    - (as_column(terms[2:3]) * grad) * res_buf[r].astype(F32)
                ).astype(BF16)
            )
        dy = dot(compact_s[...], jnp.concatenate(rows, axis=0)).astype(BF16)

        def between():
            a_take(others)
            first_pair = jnp.where(lax.div(row, 8) == 0, dmargin[0], dmargin[1])
            own_grad = jnp.where(lax.rem(lax.div(row, 4), 2) == 0, first_pair, -first_pair)
            dresidual = (as_column(by_coeff) * own_grad) * coeff - (
                as_column(by_residual) * own_grad
            ) * res_s[...]
            back_slot = iota((tokens, 16), 1)
            back = ((iota((tokens, 16), 0) == row * OWN + back_slot) & (back_slot < OWN)).astype(BF16)
            high, low = two_parts(dresidual)
            dr_s[...] = dot(back, high) + dot(back, low)

        backward_final, backward_sent = reduce(
            lambda j: dot_t(dy, dt_s[j]),
            q_s,
            qx_s,
            m1_s,
            mx_s,
            t_s,
            m2_s,
            bx_sem,
            b1_sem,
            b2_sem,
            False,
            between,
        )
        g_begin, g_take, g_end, g_sent = gather(g_s, gz_sem, gc_sem)

        @pl.when(mine)
        def _():
            g_s[z, core] = backward_final().astype(BF16)

        g_begin()
        g_take(leads + (1, -1))
        a_end()
        g_take(others[2:])
        g_end()
        total = dr_s[...]
        for j in range(TILES):
            dhidden = g_s[j].reshape(2 * HALF, TILE).astype(F32)
            factors = ab_s[j].reshape(2 * HALF, 2 * TILE).astype(F32)
            pre_grad = (jnp.concatenate([dhidden, dhidden], axis=1) * factors).astype(BF16)
            total = total + dot(pre_grad, wt_s[j])
        high, low = two_parts(total)
        by_owner = owner_s[...]
        sf_s[...] = (dot(by_owner, high) + dot(by_owner, low)).reshape(sf_s.shape)
        to_plane(lambda o: remote(sf_s.at[o], rf_s.at[row], rf_sem, 0, plane_id(o)))
        rf_s[row] = sf_s[row]
        backward_sent()
        a_sent()
        g_sent()
        wait_bytes(all_but_one(un_buf), un_sem.at[0, 0])
        wait_bytes(all_but_one(res_buf), res_sem.at[0, 0])
        wait_bytes(all_but_one(rf_s), rf_sem.at[1, 0])
        wait_bytes(all_but_one(sf_s), rf_sem.at[0, 0])

    @pl.when(mp == 1)
    def _():
        wait_bytes(rf_s, rf_sem.at[1, 0])

    grad_ref[...] = jnp.sum(rf_s[...], axis=0)[:5]
    wait_bytes(all_but_one(sum_buf), sum_sem.at[0, 0])
    wait_bytes(all_but_one(row_buf), row_sem.at[0, 0])


def local(
    text_embeds,
    image_embeds,
    offsets,
    lengths,
    loss_mask,
    norm_gain,
    unembed_rows,
    gate_up,
    down_proj,
):
    width = text_embeds.shape[1]
    units = down_proj.shape[1]
    vmem = pl.BlockSpec(memory_space=pltpu.VMEM)
    anywhere = pl.BlockSpec(memory_space=pl.ANY)
    sems = pltpu.SemaphoreType.DMA

    def half(*shape):
        return pltpu.VMEM(shape, BF16)

    def full(*shape):
        return pltpu.VMEM(shape, F32)

    def tree(units):
        return [
            half(TILES + 1, 2, HALF, units),
            half(TILES + 1, HALF, units),
            half(10, HALF, units),
            half(HALF, units),
            half(4, HALF, units),
            half(4, HALF, units),
        ]

    loss, grad = pl.pallas_call(
        kernel,
        out_shape=(jax.ShapeDtypeStruct((1, 1), F32), jax.ShapeDtypeStruct((5, width), F32)),
        in_specs=[anywhere] * 9,
        out_specs=(vmem, vmem),
        scratch_shapes=[
            half(*text_embeds.shape),
            half(*image_embeds.shape),
            pltpu.SMEM(offsets.shape, jnp.int32),
            pltpu.SMEM(lengths.shape, jnp.int32),
            pltpu.SMEM(loss_mask.shape, jnp.int32),
            half(*norm_gain.shape),
            half(*unembed_rows.shape[1:]),
            half(2, units, width),
            half(units, width),
            half(TILES + 1, 2 * TILE, width),
            half(TILES + 1, TILE, width),
            half(ROWS, 16, width),
            half(ROWS, *image_embeds.shape),
            half(ROWS, 16, width),
            half(SEQ * 4, width),
            *tree(2 * TILE),
            half(TILES, 2, HALF, TILE),
            *tree(TILE),
            half(TILES + 1, 2, HALF, 2 * TILE),
            half(TILES, 2, HALF, TILE),
            half(ROWS, 16, width),
            half(ROWS, 16, width),
            half(ROWS, 16, width),
            full(16, width),
            full(2, 128),
            full(2, 128),
            full(CHIPS, 2, 128),
            full(2 * ROWS, 4, 128),
            full(SEQ * 4, width),
            full(2 * ROWS, 8, width),
            full(ROWS, 8, width),
            half(ROWS * 16, SEQ * 4),
            half(SEQ * 4, ROWS * 16),
            half(ROWS * 16, SEQ * 4),
            sems((9,)),
            sems((2, 1)),
            sems((2, 1)),
            sems((2, 1)),
            sems((2, TILES + 1)),
            sems((2, 11)),
            sems((2, 4)),
            sems((2, 17)),
            sems((2, TILES)),
            sems((2, 17)),
            sems((2, TILES)),
            sems((2, TILES + 1)),
            sems((2, 11)),
            sems((2, 4)),
            sems((2, 17)),
            sems((2, TILES)),
            *[sems((2, 1))] * 6,
        ],
        compiler_params=pltpu.CompilerParams(
            collective_id=0, has_side_effects=True, vmem_limit_bytes=60 << 20
        ),
        name="dpo_block",
    )(
        text_embeds,
        image_embeds,
        offsets,
        lengths,
        loss_mask,
        norm_gain,
        unembed_rows[0],
        jnp.transpose(gate_up[0], (1, 2, 0)),
        down_proj[0],
    )
    return loss.reshape(()), grad


def solution(mesh):
    in_specs = (
        P("row", "col"),
        P(("mp", "row"), "col"),
        P(),
        P(),
        P("row"),
        P("mp", "col"),
        P("mp", "row", "col"),
        P("mp", "col", None, "row"),
        P("mp", "row", "col"),
    )
    out_specs = (P(), P(("mp", "row"), "col"))
    return jax.shard_map(local, mesh=mesh, in_specs=in_specs, out_specs=out_specs, check_vma=False)
```
